1024 devices in a mesh: rows: 128 (over x, z, core), cols: 8 (over y).
Axes of the slice: x: 4, y: 8, z: 16, core: 2. Of those that a mesh axis runs over, the one named last changes fastest.
Arguments:
- field: float32 [1024, 256, 128], P('rows', 'cols'), may hold values from -6 to 6
- filter_first: float32 [3, 3, 128, 128], replicated, may hold values from -0.1875 to 0.1875
- filter_second: float32 [3, 3, 128, 128], replicated, may hold values from -0.1875 to 0.1875
- cotangent: float32 [1024, 256, 128], P('rows', 'cols'), may hold values from -6 to 6
Outputs:
- input_grad: float32 [1024, 256, 128], P('rows', 'cols')
- first_grad: float32 [3, 3, 128, 128], replicated
- second_grad: float32 [3, 3, 128, 128], replicated
The draws below stay inside these ranges and needn't reach their ends.
All inputs are finite; a program needn't handle non-finite values.
Results may differ from the reference program's by a relative error of at most 0.0003.
Values sent between devices are 32-bit elements; how exact they have to be, the bound alone decides.
No kernel may reach another device: no remote copies, remote signals or barrier semaphores. Data moves between devices by JAX's collectives and lax.ppermute only.
A program may use at most 32 MiB of HBM per device.

```python
import math
import jax
import jax.numpy as jnp
from jax import lax

C = 128
HEIGHT = 1024
WIDTH = 256


def level_of(key, dims, split, smallest, largest):
    def one(axis_at, parts):
        draws = jax.random.uniform(jax.random.fold_in(jax.random.fold_in(key, 6), axis_at), (parts,), jnp.float32, smallest / len(split), largest / len(split))
        return jnp.repeat(jnp.exp(draws), dims[axis_at] // parts).reshape((-1,) + (1,) * (len(dims) - axis_at - 1))

    level = one(*split[0])
    for cut in split[1:]:
        level = level * one(*cut)
    return level


def centred(own_key, dims, deviation, most, pieces=(), kind=jnp.bfloat16):
    loudness = level_of(own_key, dims, pieces, -0.22, 0.18) if pieces else 1.0
    array = jax.random.normal(own_key, dims, jnp.float32) * deviation * loudness
    return jnp.minimum(jnp.maximum(array, -most), most).astype(kind)


def setup_inputs(seed: int = 0) -> dict:
    streams_of = jax.random.split(jax.random.key(seed), 5)
    field = centred(streams_of[0], (HEIGHT, WIDTH, C), 1.0, 6.0, ((0, 128), (1, 8)), jnp.float32)
    filter_first = centred(streams_of[1], (3, 3, C, C), (9 * C) ** -0.5, 0.1875, (), jnp.float32)
    filter_second = centred(streams_of[2], (3, 3, C, C), (9 * C) ** -0.5, 0.1875, (), jnp.float32)
    cotangent = centred(streams_of[3], (HEIGHT, WIDTH, C), 1.0, 6.0, ((0, 128), (1, 8)), jnp.float32)
    return {"field": field, "filter_first": filter_first, "filter_second": filter_second, "cotangent": cotangent}


def conv_layer(source, kernel):
    return lax.conv_general_dilated(source[None], kernel, (1, 1), ((1, 1), (1, 1)), dimension_numbers=('NHWC', 'HWIO', 'NHWC'), precision=lax.Precision.HIGHEST)[0]

def forward(field, filter_first, filter_second):
    hidden = jax.nn.silu(conv_layer(field, filter_first))
    return jax.nn.silu(conv_layer(hidden, filter_second))

def reference(field, filter_first, filter_second, cotangent):
    output, pullback = jax.vjp(forward, field, filter_first, filter_second)
    grads = pullback(cotangent)
    factor = 1.0 / math.sqrt(HEIGHT * WIDTH)
    return (grads[0], grads[1] * factor, grads[2] * factor)
```

```python
import math

import jax
import jax.numpy as jnp
from jax import lax
from jax.sharding import Mesh, PartitionSpec as P

ROWS = ("x", "z", "core")
FIELD_HALO = 4
COT_HALO = 2


def neighbours(values, axis):
    count = lax.axis_size(axis)
    forward = [(i, i + 1) for i in range(count - 1)]
    backward = [(target, source) for source, target in forward]
    low, high = values
    return lax.ppermute(low, axis, forward), lax.ppermute(high, axis, backward)


def wide_halo(field, cotangent):
    tile_rows, tile_cols, channels = field.shape
    a, b = FIELD_HALO, COT_HALO
    low, high = neighbours(
        (
            jnp.concatenate([field[-a:], cotangent[-b:]], axis=0),
            jnp.concatenate([field[:a], cotangent[:b]], axis=0),
        ),
        ROWS,
    )
    field = jnp.concatenate([low[:a], field, high[:a]], axis=0)
    cotangent = jnp.concatenate([low[a:], cotangent, high[a:]], axis=0)
    rows_f, rows_c = field.shape[0], cotangent.shape[0]

    def pack(f, c):
        return jnp.concatenate([f.reshape(-1, channels), c.reshape(-1, channels)], axis=0)

    low, high = neighbours(
        (pack(field[:, -a:], cotangent[:, -b:]), pack(field[:, :a], cotangent[:, :b])), "y"
    )

    def unpack(p):
        return p[: rows_f * a].reshape(rows_f, a, channels), p[rows_f * a :].reshape(rows_c, b, channels)

    low_f, low_c = unpack(low)
    high_f, high_c = unpack(high)
    field = jnp.concatenate([low_f, field, high_f], axis=1)
    cotangent = jnp.concatenate([low_c, cotangent, high_c], axis=1)
    return field, cotangent


def shifted_product(padded, kernel):
    out_rows = padded.shape[0] - 2
    out_cols = padded.shape[1] - 2
    summed = None
    for row_shift in range(3):
        stripe = padded[row_shift : row_shift + out_rows]
        stacked = jnp.concatenate(
            [stripe[:, col_shift : col_shift + out_cols] for col_shift in range(3)], axis=2
        )
        partial_sum = jnp.dot(
            stacked.reshape(out_rows * out_cols, -1),
            kernel[row_shift].reshape(-1, kernel.shape[3]),
            precision=lax.Precision.HIGH,
            preferred_element_type=jnp.float32,
        )
        summed = partial_sum if summed is None else summed + partial_sum
    return summed.reshape(out_rows, out_cols, -1)


def flipped(kernel):
    return jnp.transpose(jnp.flip(kernel, (0, 1)), (0, 1, 3, 2))


def filter_product(padded, deltas):
    out_rows, out_cols, channels = deltas.shape
    flat_delta = deltas.reshape(out_rows * out_cols, channels)
    outer = []
    for row_shift in range(3):
        for col_shift in range(3):
            window = padded[
                row_shift : row_shift + out_rows, col_shift : col_shift + out_cols
            ].reshape(out_rows * out_cols, -1)
            outer.append(
                lax.dot_general(
                    window,
                    flat_delta,
                    (((0,), (0,)), ((), ())),
                    precision=lax.Precision.HIGH,
                    preferred_element_type=jnp.float32,
                )
            )
    return jnp.concatenate(outer, axis=0)


def silu_slope(values):
    sigmoid = jax.nn.sigmoid(values)
    return sigmoid * (1.0 + values * (1.0 - sigmoid))


def inside(tile_rows, tile_cols, margin):
    height = tile_rows * lax.axis_size(ROWS)
    width = tile_cols * lax.axis_size("y")
    shape = (tile_rows + 2 * margin, tile_cols + 2 * margin, 1)
    row = lax.broadcasted_iota(jnp.int32, shape, 0) + lax.axis_index(ROWS) * tile_rows - margin
    col = lax.broadcasted_iota(jnp.int32, shape, 1) + lax.axis_index("y") * tile_cols - margin
    return (row >= 0) & (row < height) & (col >= 0) & (col < width)


def total(first, second):
    core = lax.axis_index("core")
    other = [(0, 1), (1, 0)]
    mine = jnp.where(core == 0, second, first)
    theirs = jnp.where(core == 0, first, second)
    with jax.named_scope("cores"):
        mine = mine + lax.ppermute(theirs, "core", other)
    channels = mine.shape[-1]
    with jax.named_scope("x_scatter"):
        n = lax.axis_size("x")
        mine = lax.all_to_all(mine.reshape(n, -1, channels), "x", 0, 0).sum(0)
    with jax.named_scope("y_scatter"):
        n = lax.axis_size("y")
        mine = lax.all_to_all(mine.reshape(n, -1, channels), "y", 0, 0).sum(0)
    with jax.named_scope("z_total"):
        mine = lax.all_gather(mine, "z", axis=0).sum(0)
    with jax.named_scope("y_gather"):
        mine = lax.all_gather(mine, "y", axis=0).reshape(-1, channels)
    with jax.named_scope("x_gather"):
        mine = lax.all_gather(mine, "x", axis=0).reshape(-1, channels)
    with jax.named_scope("cores_back"):
        theirs = lax.ppermute(mine, "core", other)
    first = jnp.where(core == 0, theirs, mine)
    second = jnp.where(core == 0, mine, theirs)
    return first, second


def local(field, filter_first, filter_second, cotangent):
    tile_rows, tile_cols, channels = field.shape
    pixels = tile_rows * tile_cols * lax.axis_size(ROWS) * lax.axis_size("y")
    factor = 1.0 / math.sqrt(pixels)
    far_field, far_cot = wide_halo(field, cotangent)
    first_pre = shifted_product(far_field, filter_first)
    hidden = jnp.where(inside(tile_rows, tile_cols, 3), jax.nn.silu(first_pre), 0.0)
    second_pre = shifted_product(hidden, filter_second)
    second_delta = far_cot * silu_slope(second_pre)
    back_pre = shifted_product(second_delta, flipped(filter_second))
    first_delta = back_pre * silu_slope(first_pre[2:-2, 2:-2])
    first_delta = jnp.where(inside(tile_rows, tile_cols, 1), first_delta, 0.0)
    second_grad = filter_product(hidden[2:-2, 2:-2], second_delta[2:-2, 2:-2]) * factor
    first_grad = filter_product(far_field[3:-3, 3:-3], first_delta[1:-1, 1:-1]) * factor
    first_grad, second_grad = total(first_grad, second_grad)
    input_grad = shifted_product(first_delta, flipped(filter_first))
    shape = filter_first.shape
    return (input_grad, first_grad.reshape(shape), second_grad.reshape(shape))


def solution(mesh):
    fine = Mesh(mesh.devices.reshape(4, 16, 2, 8), ("x", "z", "core", "y"))
    tile = P(ROWS, "y", None)
    return jax.shard_map(
        local, mesh=fine, in_specs=(tile, P(), P(), tile), out_specs=(tile, P(), P()), check_vma=False
    )
```

```python
import math

import jax
import jax.numpy as jnp
from jax import lax
from jax.sharding import Mesh, PartitionSpec as P

ROWS = ("x", "z", "core")
FIELD_HALO = 4
COT_HALO = 2


def neighbours(values, axis):
    count = lax.axis_size(axis)
    forward = [(i, i + 1) for i in range(count - 1)]
    backward = [(target, source) for source, target in forward]
    low, high = values
    return lax.ppermute(low, axis, forward), lax.ppermute(high, axis, backward)


def wide_halo(field, cotangent):
    tile_rows, tile_cols, channels = field.shape
    a, b = FIELD_HALO, COT_HALO
    low, high = neighbours(
        (
            jnp.concatenate([field[-a:], cotangent[-b:]], axis=0),
            jnp.concatenate([field[:a], cotangent[:b]], axis=0),
        ),
        ROWS,
    )
    field = jnp.concatenate([low[:a], field, high[:a]], axis=0)
    cotangent = jnp.concatenate([low[a:], cotangent, high[a:]], axis=0)
    rows_f, rows_c = field.shape[0], cotangent.shape[0]

    def pack(f, c):
        return jnp.concatenate([f.reshape(-1, channels), c.reshape(-1, channels)], axis=0)

    low, high = neighbours(
        (pack(field[:, -a:], cotangent[:, -b:]), pack(field[:, :a], cotangent[:, :b])), "y"
    )

    def unpack(p):
        return p[: rows_f * a].reshape(rows_f, a, channels), p[rows_f * a :].reshape(rows_c, b, channels)

    low_f, low_c = unpack(low)
    high_f, high_c = unpack(high)
    field = jnp.concatenate([low_f, field, high_f], axis=1)
    cotangent = jnp.concatenate([low_c, cotangent, high_c], axis=1)
    return field, cotangent


def shifted_product(padded, kernel):
    out_rows = padded.shape[0] - 2
    out_cols = padded.shape[1] - 2
    summed = None
    for row_shift in range(3):
        stripe = padded[row_shift : row_shift + out_rows]
        stacked = jnp.concatenate(
            [stripe[:, col_shift : col_shift + out_cols] for col_shift in range(3)], axis=2
        )
        partial_sum = jnp.dot(
            stacked.reshape(out_rows * out_cols, -1),
            kernel[row_shift].reshape(-1, kernel.shape[3]),
            precision=lax.Precision.HIGH,
            preferred_element_type=jnp.float32,
        )
        summed = partial_sum if summed is None else summed + partial_sum
    return summed.reshape(out_rows, out_cols, -1)


def flipped(kernel):
    return jnp.transpose(jnp.flip(kernel, (0, 1)), (0, 1, 3, 2))


def filter_product(padded, deltas):
    out_rows, out_cols, channels = deltas.shape
    flat_delta = deltas.reshape(out_rows * out_cols, channels)
    outer = []
    for row_shift in range(3):
        for col_shift in range(3):
            window = padded[
                row_shift : row_shift + out_rows, col_shift : col_shift + out_cols
            ].reshape(out_rows * out_cols, -1)
            outer.append(
                lax.dot_general(
                    window,
                    flat_delta,
                    (((0,), (0,)), ((), ())),
                    precision=lax.Precision.HIGH,
                    preferred_element_type=jnp.float32,
                )
            )
    return jnp.concatenate(outer, axis=0)


def silu_slope(values):
    sigmoid = jax.nn.sigmoid(values)
    return sigmoid * (1.0 + values * (1.0 - sigmoid))


def inside(tile_rows, tile_cols, margin):
    height = tile_rows * lax.axis_size(ROWS)
    width = tile_cols * lax.axis_size("y")
    shape = (tile_rows + 2 * margin, tile_cols + 2 * margin, 1)
    row = lax.broadcasted_iota(jnp.int32, shape, 0) + lax.axis_index(ROWS) * tile_rows - margin
    col = lax.broadcasted_iota(jnp.int32, shape, 1) + lax.axis_index("y") * tile_cols - margin
    return (row >= 0) & (row < height) & (col >= 0) & (col < width)


def to_all(values, axis):
    copies = jnp.broadcast_to(values[None], (lax.axis_size(axis),) + values.shape)
    return lax.all_to_all(copies, axis, 0, 0)


def total(first, second):
    core = lax.axis_index("core")
    other = [(0, 1), (1, 0)]
    mine = jnp.where(core == 0, second, first)
    theirs = jnp.where(core == 0, first, second)
    with jax.named_scope("cores"):
        mine = mine + lax.ppermute(theirs, "core", other)
    channels = mine.shape[-1]
    with jax.named_scope("xy_scatter"):
        n = lax.axis_size(("x", "y"))
        mine = lax.all_to_all(mine.reshape(n, -1, channels), ("x", "y"), 0, 0).sum(0)
    with jax.named_scope("z_total"):
        mine = to_all(mine, "z").sum(0)
    with jax.named_scope("xy_gather"):
        mine = to_all(mine, ("x", "y")).reshape(-1, channels)
    with jax.named_scope("cores_back"):
        theirs = lax.ppermute(mine, "core", other)
    first = jnp.where(core == 0, theirs, mine)
    second = jnp.where(core == 0, mine, theirs)
    return first, second


def local(field, filter_first, filter_second, cotangent):
    tile_rows, tile_cols, channels = field.shape
    pixels = tile_rows * tile_cols * lax.axis_size(ROWS) * lax.axis_size("y")
    factor = 1.0 / math.sqrt(pixels)
    far_field, far_cot = wide_halo(field, cotangent)
    first_pre = shifted_product(far_field, filter_first)
    hidden = jnp.where(inside(tile_rows, tile_cols, 3), jax.nn.silu(first_pre), 0.0)
    second_pre = shifted_product(hidden, filter_second)
    second_delta = far_cot * silu_slope(second_pre)
    back_pre = shifted_product(second_delta, flipped(filter_second))
    first_delta = back_pre * silu_slope(first_pre[2:-2, 2:-2])
    first_delta = jnp.where(inside(tile_rows, tile_cols, 1), first_delta, 0.0)
    second_grad = filter_product(hidden[2:-2, 2:-2], second_delta[2:-2, 2:-2]) * factor
    first_grad = filter_product(far_field[3:-3, 3:-3], first_delta[1:-1, 1:-1]) * factor
    first_grad, second_grad = total(first_grad, second_grad)
    input_grad = shifted_product(first_delta, flipped(filter_first))
    shape = filter_first.shape
    return (input_grad, first_grad.reshape(shape), second_grad.reshape(shape))


def solution(mesh):
    fine = Mesh(mesh.devices.reshape(4, 16, 2, 8), ("x", "z", "core", "y"))
    tile = P(ROWS, "y", None)
    return jax.shard_map(
        local, mesh=fine, in_specs=(tile, P(), P(), tile), out_specs=(tile, P(), P()), check_vma=False
    )
```

```python
import functools
import math

import jax
import jax.numpy as jnp
from jax import lax
from jax.experimental import pallas as pl
from jax.experimental.pallas import tpu as pltpu
from jax.sharding import Mesh, PartitionSpec as P

ROWS = ("x", "z", "core")
FIELD_HALO = 4
COT_HALO = 2
PITCH = 48
LEFT = 8
SLACK = 8
VMEM_LIMIT = 40 * 2**20
PARAMS = pltpu.CompilerParams(vmem_limit_bytes=VMEM_LIMIT)
IN_VMEM = pl.BlockSpec(memory_space=pltpu.VMEM)
IN_SMEM = pl.BlockSpec(memory_space=pltpu.SMEM)


def neighbours(values, axis):
    count = lax.axis_size(axis)
    forward = [(i, i + 1) for i in range(count - 1)]
    backward = [(target, source) for source, target in forward]
    low, high = values
    return lax.ppermute(low, axis, forward), lax.ppermute(high, axis, backward)


def image(rows, dtype=jnp.float32):
    return pltpu.VMEM((2 * SLACK + rows * PITCH, 128), dtype)


def spot(row, col):
    return SLACK + row * PITCH + col


def pack_kernel(field, cot, low, high, to_low, to_high):
    a, b = FIELD_HALO, COT_HALO
    tile_rows, tile_cols, _ = field.shape
    for out, col_a, col_b in ((to_low, 0, 0), (to_high, tile_cols - a, tile_cols - b)):
        at = 0
        for part, rows, col, count in (
            (low, range(a), col_a, a),
            (field, range(tile_rows), col_a, a),
            (high, range(a), col_a, a),
            (low, range(a, a + b), col_b, b),
            (cot, range(tile_rows), col_b, b),
            (high, range(a, a + b), col_b, b),
        ):
            for row in rows:
                out[at : at + count, :] = part[row, col : col + count, :]
                at += count


def split(values):
    high = values.astype(jnp.bfloat16)
    low = (values - high.astype(jnp.float32)).astype(jnp.bfloat16)
    return high, low


def load_filter(source, flip, both, first):
    for a in range(3):
        if flip:
            taps = jnp.concatenate([source[2 - a, 2 - b] for b in range(3)], axis=1)
        else:
            taps = source[a].reshape(-1, source.shape[3])
        high, low = split(taps)
        both[a] = jnp.concatenate([high, low], axis=0 if flip else 1)
        first[a] = high


def convolve(source, rows, flip, both, first, high, low):
    taken = (rows + 2) * PITCH
    made = rows * PITCH
    shifts = [source[SLACK - 1 + b : SLACK - 1 + b + taken, :] for b in range(3)]
    for b in range(3):
        part_high, part_low = split(shifts[b])
        high[0:taken, 128 * b : 128 * b + 128] = part_high
        low[0:taken, 128 * b : 128 * b + 128] = part_low
    dims = (((1,), (1 if flip else 0,)), ((), ()))
    wide = None
    thin = None
    for a in range(3):
        start = a * PITCH
        p = lax.dot_general(
            high[start : start + made, :], both[a], dims, preferred_element_type=jnp.float32
        )
        q = lax.dot_general(
            low[start : start + made, :], first[a], dims, preferred_element_type=jnp.float32
        )
        wide = p if wide is None else wide + p
        thin = q if thin is None else thin + q
    return wide[:, :128] + wide[:, 128:] + thin


def filter_product(values, value_row, deltas, delta_row, tile_rows, tile_cols, factor):
    rows = tile_rows + 2
    windows = []
    for b in range(3):
        col = LEFT - 1 + b
        windows.append(
            jnp.concatenate(
                [
                    values[spot(value_row + r, col) : spot(value_row + r, col) + tile_cols, :]
                    for r in range(rows)
                ],
                axis=0,
            )
        )
    high, low = split(jnp.concatenate(windows, axis=1))
    delta = jnp.concatenate(
        [
            deltas[spot(delta_row + r, LEFT) : spot(delta_row + r, LEFT) + tile_cols, :]
            for r in range(tile_rows)
        ],
        axis=0,
    )
    delta_high, delta_low = split((delta * factor).T)
    pixels = tile_rows * tile_cols
    outs = []
    for a in range(3):
        start = a * tile_cols
        window = high[start : start + pixels]
        out = jnp.dot(delta_high, window, preferred_element_type=jnp.float32)
        out += jnp.dot(
            delta_high, low[start : start + pixels], preferred_element_type=jnp.float32
        )
        out += jnp.dot(delta_low, window, preferred_element_type=jnp.float32)
        outs.append(out.T)
    return jnp.concatenate(outs, axis=0)


def inside(place, rows, margin, tile_rows, tile_cols, height, width):
    shape = (rows, PITCH, 128)
    row = lax.broadcasted_iota(jnp.int32, shape, 0) + (place[0] * tile_rows - margin)
    col = lax.broadcasted_iota(jnp.int32, shape, 1) + (place[1] * tile_cols - LEFT)
    keep = (row >= 0) & (row < height) & (col >= 0) & (col < width)
    return jnp.where(keep, 1.0, 0.0).reshape(rows * PITCH, 128) > 0.5


def main_kernel(
    height, width, place, field, cot, low, high, from_low, from_high, filter_first, filter_second,
    kept, sent, first_delta_out,
    field_image, cot_image, hidden_image, slope_image, delta_image,
    both, first, both_back, first_back, part_high, part_low,
):
    a, b = FIELD_HALO, COT_HALO
    tile_rows, tile_cols, _ = field.shape
    for target, own, halo, base, offset in (
        (field_image, field, a, 0, 0),
        (cot_image, cot, b, a, (tile_rows + 2 * a) * a),
    ):
        for row in range(tile_rows + 2 * halo):
            if row < halo:
                line = low[base + row]
            elif row < halo + tile_rows:
                line = own[row - halo]
            else:
                line = high[base + row - halo - tile_rows]
            target[spot(row, LEFT) : spot(row, LEFT) + tile_cols, :] = line
            left = spot(row, LEFT - halo)
            target[left : left + halo, :] = from_low[offset + row * halo : offset + row * halo + halo, :]
            right = spot(row, LEFT + tile_cols)
            target[right : right + halo, :] = from_high[
                offset + row * halo : offset + row * halo + halo, :
            ]
    grid = (tile_rows, tile_cols, height, width)
    factor = 1.0 / math.sqrt(height * width)
    core = place[2]

    rows = tile_rows + 6
    load_filter(filter_first, False, both.at[0], first.at[0])
    pre = convolve(field_image, rows, False, both.at[0], first.at[0], part_high, part_low)
    sigmoid = jax.nn.sigmoid(pre)
    slope_image[SLACK : SLACK + rows * PITCH, :] = sigmoid * (1.0 + pre * (1.0 - sigmoid))
    hidden_image[SLACK : SLACK + rows * PITCH, :] = jnp.where(
        inside(place, rows, 3, *grid), pre * sigmoid, 0.0
    )

    rows = tile_rows + 4
    load_filter(filter_second, False, both.at[1], first.at[1])
    pre = convolve(hidden_image, rows, False, both.at[1], first.at[1], part_high, part_low)
    sigmoid = jax.nn.sigmoid(pre)
    delta_image[SLACK : SLACK + rows * PITCH, :] = cot_image[SLACK : SLACK + rows * PITCH, :] * (
        sigmoid * (1.0 + pre * (1.0 - sigmoid))
    )
    grad = filter_product(hidden_image, 2, delta_image, 2, tile_rows, tile_cols, factor)

    @pl.when(core == 0)
    def _():
        kept[...] = grad

    @pl.when(core != 0)
    def _():
        sent[...] = grad

    rows = tile_rows + 2
    load_filter(filter_second, True, both_back, first_back)
    back = convolve(delta_image, rows, True, both_back, first_back, part_high, part_low)
    start = spot(2, 0)
    first_delta_out[SLACK : SLACK + rows * PITCH, :] = jnp.where(
        inside(place, rows, 1, *grid), back * slope_image[start : start + rows * PITCH, :], 0.0
    )
    grad = filter_product(field_image, 3, first_delta_out, 1, tile_rows, tile_cols, factor)

    @pl.when(core == 0)
    def _():
        sent[...] = grad

    @pl.when(core != 0)
    def _():
        kept[...] = grad


def input_kernel(first_delta, filter_first, input_grad, both_back, first_back, part_high, part_low):
    tile_rows, tile_cols, _ = input_grad.shape
    load_filter(filter_first, True, both_back, first_back)
    out = convolve(first_delta, tile_rows, True, both_back, first_back, part_high, part_low)
    for row in range(tile_rows):
        start = row * PITCH + LEFT
        input_grad[row] = out[start : start + tile_cols]


def filters_scratch(flip):
    if flip:
        return [pltpu.VMEM((3, 256, 384), jnp.bfloat16), pltpu.VMEM((3, 128, 384), jnp.bfloat16)]
    return [pltpu.VMEM((2, 3, 384, 256), jnp.bfloat16), pltpu.VMEM((2, 3, 384, 128), jnp.bfloat16)]


def parts_scratch(rows):
    return [pltpu.VMEM((rows * PITCH, 384), jnp.bfloat16)] * 2


def to_all(values, axis):
    copies = jnp.broadcast_to(values[None], (lax.axis_size(axis),) + values.shape)
    return lax.all_to_all(copies, axis, 0, 0)


def total(mine, theirs):
    core = lax.axis_index("core")
    other = [(0, 1), (1, 0)]
    with jax.named_scope("cores"):
        mine = mine + lax.ppermute(theirs, "core", other)
    channels = mine.shape[-1]
    with jax.named_scope("xy_scatter"):
        n = lax.axis_size(("x", "y"))
        mine = lax.all_to_all(mine.reshape(n, -1, channels), ("x", "y"), 0, 0).sum(0)
    with jax.named_scope("z_total"):
        mine = to_all(mine, "z").sum(0)
    with jax.named_scope("xy_gather"):
        mine = to_all(mine, ("x", "y")).reshape(-1, channels)
    with jax.named_scope("cores_back"):
        theirs = lax.ppermute(mine, "core", other)
    first = jnp.where(core == 0, theirs, mine)
    second = jnp.where(core == 0, mine, theirs)
    return first, second


def local(field, filter_first, filter_second, cotangent):
    tile_rows, tile_cols, channels = field.shape
    a, b = FIELD_HALO, COT_HALO
    height = tile_rows * lax.axis_size(ROWS)
    width = tile_cols * lax.axis_size("y")
    place = jnp.stack([lax.axis_index(ROWS), lax.axis_index("y"), lax.axis_index("core")])
    place = place.astype(jnp.int32)
    low, high = neighbours(
        (
            jnp.concatenate([field[-a:], cotangent[-b:]], axis=0),
            jnp.concatenate([field[:a], cotangent[:b]], axis=0),
        ),
        ROWS,
    )
    lines = (tile_rows + 2 * a) * a + (tile_rows + 2 * b) * b
    side = jax.ShapeDtypeStruct((lines, channels), jnp.float32)
    to_low, to_high = pl.pallas_call(
        pack_kernel,
        out_shape=(side, side),
        in_specs=[IN_VMEM] * 4,
        out_specs=(IN_VMEM, IN_VMEM),
        compiler_params=PARAMS,
        name="pack_sides",
    )(field, cotangent, low, high)
    from_low, from_high = neighbours((to_high, to_low), "y")
    grad = jax.ShapeDtypeStruct((9 * channels, channels), jnp.float32)
    delta_rows = tile_rows + 2
    kept, sent, first_delta = pl.pallas_call(
        functools.partial(main_kernel, height, width),
        out_shape=(
            grad,
            grad,
            jax.ShapeDtypeStruct((2 * SLACK + delta_rows * PITCH, channels), jnp.float32),
        ),
        in_specs=[IN_SMEM] + [IN_VMEM] * 8,
        out_specs=(IN_VMEM, IN_VMEM, IN_VMEM),
        scratch_shapes=[
            image(tile_rows + 2 * a),
            image(tile_rows + 2 * b),
            image(tile_rows + 6),
            image(tile_rows + 6),
            image(tile_rows + 4),
            *filters_scratch(False),
            *filters_scratch(True),
            *parts_scratch(tile_rows + 2 * a),
        ],
        compiler_params=PARAMS,
        name="gradients",
    )(place, field, cotangent, low, high, from_low, from_high, filter_first, filter_second)
    first_grad, second_grad = total(kept, sent)
    input_grad = pl.pallas_call(
        input_kernel,
        out_shape=jax.ShapeDtypeStruct(field.shape, jnp.float32),
        in_specs=[IN_VMEM] * 2,
        out_specs=IN_VMEM,
        scratch_shapes=[*filters_scratch(True), *parts_scratch(delta_rows)],
        compiler_params=PARAMS,
        cost_estimate=pl.CostEstimate(flops=2 * 10**9, bytes_accessed=10**6, transcendentals=0),
        name="input_grad",
    )(first_delta, filter_first)
    shape = filter_first.shape
    return (input_grad, first_grad.reshape(shape), second_grad.reshape(shape))


def solution(mesh):
    fine = Mesh(mesh.devices.reshape(4, 16, 2, 8), ("x", "z", "core", "y"))
    tile = P(ROWS, "y", None)
    return jax.shard_map(
        local, mesh=fine, in_specs=(tile, P(), P(), tile), out_specs=(tile, P(), P()), check_vma=False
    )
```

```python
import functools
import math

import jax
import jax.numpy as jnp
from jax import lax
from jax.experimental import pallas as pl
from jax.experimental.pallas import tpu as pltpu
from jax.sharding import Mesh, PartitionSpec as P

ROWS = ("x", "zh", "zl", "core")
FIELD_HALO = 4
COT_HALO = 2
PITCH = 48
LEFT = 8
SLACK = 8
VMEM_LIMIT = 24 * 2**20
PARAMS = pltpu.CompilerParams(vmem_limit_bytes=VMEM_LIMIT)
IN_VMEM = pl.BlockSpec(memory_space=pltpu.VMEM)
IN_SMEM = pl.BlockSpec(memory_space=pltpu.SMEM)


def neighbours(values, axis):
    count = lax.axis_size(axis)
    forward = [(i, i + 1) for i in range(count - 1)]
    backward = [(target, source) for source, target in forward]
    low, high = values
    return lax.ppermute(low, axis, forward), lax.ppermute(high, axis, backward)


def image(rows, dtype=jnp.float32):
    return pltpu.VMEM((2 * SLACK + rows * PITCH, 128), dtype)


def spot(row, col):
    return SLACK + row * PITCH + col


def pack_kernel(field, cot, low, high, to_low, to_high):
    a, b = FIELD_HALO, COT_HALO
    tile_rows, tile_cols, _ = field.shape
    for out, col_a, col_b in ((to_low, 0, 0), (to_high, tile_cols - a, tile_cols - b)):
        at = 0
        for part, rows, col, count in (
            (low, range(a), col_a, a),
            (field, range(tile_rows), col_a, a),
            (high, range(a), col_a, a),
            (low, range(a, a + b), col_b, b),
            (cot, range(tile_rows), col_b, b),
            (high, range(a, a + b), col_b, b),
        ):
            for row in rows:
                out[at : at + count, :] = part[row, col : col + count, :]
                at += count


def split(values):
    high = values.astype(jnp.bfloat16)
    low = (values - high.astype(jnp.float32)).astype(jnp.bfloat16)
    return high, low


def filters_kernel(filter_first, filter_second, forward, back):
    for layer, source in enumerate((filter_first, filter_second)):
        for a in range(3):
            taps = source[a].reshape(-1, source.shape[3])
            forward[layer, a] = jnp.concatenate(split(taps), axis=1)
            taps = jnp.concatenate([source[2 - a, 2 - b] for b in range(3)], axis=1)
            back[layer, a] = jnp.concatenate(split(taps), axis=0)


def convolve(source, rows, flip, both, high, low):
    taken = (rows + 2) * PITCH
    made = rows * PITCH
    shifts = [source[SLACK - 1 + b : SLACK - 1 + b + taken, :] for b in range(3)]
    for b in range(3):
        part_high, part_low = split(shifts[b])
        high[0:taken, 128 * b : 128 * b + 128] = part_high
        low[0:taken, 128 * b : 128 * b + 128] = part_low
    dims = (((1,), (1 if flip else 0,)), ((), ()))
    wide = None
    thin = None
    for a in range(3):
        start = a * PITCH
        p = lax.dot_general(
            high[start : start + made, :], both[a], dims, preferred_element_type=jnp.float32
        )
        q = lax.dot_general(
            low[start : start + made, :],
            both[a, :128] if flip else both[a, :, :128],
            dims,
            preferred_element_type=jnp.float32,
        )
        wide = p if wide is None else wide + p
        thin = q if thin is None else thin + q
    return wide[:, :128] + wide[:, 128:] + thin


def filter_product(values, value_row, deltas, delta_row, tile_rows, tile_cols, factor):
    rows = tile_rows + 2
    windows = []
    for b in range(3):
        col = LEFT - 1 + b
        windows.append(
            jnp.concatenate(
                [
                    values[spot(value_row + r, col) : spot(value_row + r, col) + tile_cols, :]
                    for r in range(rows)
                ],
                axis=0,
            )
        )
    high, low = split(jnp.concatenate(windows, axis=1))
    delta = jnp.concatenate(
        [
            deltas[spot(delta_row + r, LEFT) : spot(delta_row + r, LEFT) + tile_cols, :]
            for r in range(tile_rows)
        ],
        axis=0,
    )
    delta_high, delta_low = split((delta * factor).T)
    pixels = tile_rows * tile_cols
    outs = []
    for a in range(3):
        start = a * tile_cols
        window = high[start : start + pixels]
        out = jnp.dot(delta_high, window, preferred_element_type=jnp.float32)
        out += jnp.dot(
            delta_high, low[start : start + pixels], preferred_element_type=jnp.float32
        )
        out += jnp.dot(delta_low, window, preferred_element_type=jnp.float32)
        outs.append(out.T)
    return jnp.concatenate(outs, axis=0)


def inside(place, rows, margin, tile_rows, tile_cols, height, width):
    shape = (rows, PITCH, 128)
    row = lax.broadcasted_iota(jnp.int32, shape, 0) + (place[0] * tile_rows - margin)
    col = lax.broadcasted_iota(jnp.int32, shape, 1) + (place[1] * tile_cols - LEFT)
    keep = (row >= 0) & (row < height) & (col >= 0) & (col < width)
    return jnp.where(keep, 1.0, 0.0).reshape(rows * PITCH, 128) > 0.5


def main_kernel(
    height, width, place, field, cot, low, high, from_low, from_high, forward, backward,
    kept, sent, first_delta_out,
    field_image, cot_image, hidden_image, slope_image, delta_image,
    part_high, part_low,
):
    a, b = FIELD_HALO, COT_HALO
    tile_rows, tile_cols, _ = field.shape
    for target, own, halo, base, offset in (
        (field_image, field, a, 0, 0),
        (cot_image, cot, b, a, (tile_rows + 2 * a) * a),
    ):
        for row in range(tile_rows + 2 * halo):
            if row < halo:
                line = low[base + row]
            elif row < halo + tile_rows:
                line = own[row - halo]
            else:
                line = high[base + row - halo - tile_rows]
            target[spot(row, LEFT) : spot(row, LEFT) + tile_cols, :] = line
            left = spot(row, LEFT - halo)
            target[left : left + halo, :] = from_low[offset + row * halo : offset + row * halo + halo, :]
            right = spot(row, LEFT + tile_cols)
            target[right : right + halo, :] = from_high[
                offset + row * halo : offset + row * halo + halo, :
            ]
    grid = (tile_rows, tile_cols, height, width)
    factor = 1.0 / math.sqrt(height * width)
    core = place[2]

    rows = tile_rows + 6
    pre = convolve(field_image, rows, False, forward.at[0], part_high, part_low)
    sigmoid = jax.nn.sigmoid(pre)
    slope_image[SLACK : SLACK + rows * PITCH, :] = sigmoid * (1.0 + pre * (1.0 - sigmoid))
    hidden_image[SLACK : SLACK + rows * PITCH, :] = jnp.where(
        inside(place, rows, 3, *grid), pre * sigmoid, 0.0
    )

    rows = tile_rows + 4
    pre = convolve(hidden_image, rows, False, forward.at[1], part_high, part_low)
    sigmoid = jax.nn.sigmoid(pre)
    delta_image[SLACK : SLACK + rows * PITCH, :] = cot_image[SLACK : SLACK + rows * PITCH, :] * (
        sigmoid * (1.0 + pre * (1.0 - sigmoid))
    )
    grad = filter_product(hidden_image, 2, delta_image, 2, tile_rows, tile_cols, factor)

    @pl.when(core == 0)
    def _():
        kept[...] = grad

    @pl.when(core != 0)
    def _():
        sent[...] = grad

    rows = tile_rows + 2
    back = convolve(delta_image, rows, True, backward.at[1], part_high, part_low)
    start = spot(2, 0)
    first_delta_out[SLACK : SLACK + rows * PITCH, :] = jnp.where(
        inside(place, rows, 1, *grid), back * slope_image[start : start + rows * PITCH, :], 0.0
    )
    grad = filter_product(field_image, 3, first_delta_out, 1, tile_rows, tile_cols, factor)

    @pl.when(core == 0)
    def _():
        sent[...] = grad

    @pl.when(core != 0)
    def _():
        kept[...] = grad


def input_kernel(first_delta, backward, input_grad, part_high, part_low):
    tile_rows, tile_cols, _ = input_grad.shape
    out = convolve(first_delta, tile_rows, True, backward.at[0], part_high, part_low)
    for row in range(tile_rows):
        start = row * PITCH + LEFT
        input_grad[row] = out[start : start + tile_cols]


def parts_scratch(rows):
    return [pltpu.VMEM((rows * PITCH, 384), jnp.bfloat16)] * 2


def to_all(values, axis):
    copies = jnp.broadcast_to(values[None], (lax.axis_size(axis),) + values.shape)
    return lax.all_to_all(copies, axis, 0, 0)


def total(mine, theirs):
    core = lax.axis_index("core")
    other = [(0, 1), (1, 0)]
    with jax.named_scope("cores"):
        mine = mine + lax.ppermute(theirs, "core", other)
    channels = mine.shape[-1]
    with jax.named_scope("xy_scatter"):
        n = lax.axis_size(("x", "y"))
        mine = lax.all_to_all(mine.reshape(n, -1, channels), ("x", "y"), 0, 0).sum(0)
    with jax.named_scope("z_total"):
        mine = to_all(mine, "zl").sum(0)
        mine = to_all(mine, "zh").sum(0)
    with jax.named_scope("xy_gather"):
        mine = to_all(mine, ("x", "y")).reshape(-1, channels)
    with jax.named_scope("cores_back"):
        theirs = lax.ppermute(mine, "core", other)
    first = jnp.where(core == 0, theirs, mine)
    second = jnp.where(core == 0, mine, theirs)
    return first, second


def local(field, filter_first, filter_second, cotangent):
    tile_rows, tile_cols, channels = field.shape
    a, b = FIELD_HALO, COT_HALO
    height = tile_rows * lax.axis_size(ROWS)
    width = tile_cols * lax.axis_size("y")
    place = jnp.stack([lax.axis_index(ROWS), lax.axis_index("y"), lax.axis_index("core")])
    place = place.astype(jnp.int32)
    low, high = neighbours(
        (
            jnp.concatenate([field[-a:], cotangent[-b:]], axis=0),
            jnp.concatenate([field[:a], cotangent[:b]], axis=0),
        ),
        ROWS,
    )
    forward, backward = pl.pallas_call(
        filters_kernel,
        out_shape=(
            jax.ShapeDtypeStruct((2, 3, 3 * channels, 2 * channels), jnp.bfloat16),
            jax.ShapeDtypeStruct((2, 3, 2 * channels, 3 * channels), jnp.bfloat16),
        ),
        in_specs=[IN_VMEM] * 2,
        out_specs=(IN_VMEM, IN_VMEM),
        compiler_params=PARAMS,
        cost_estimate=pl.CostEstimate(flops=2 * 10**9, bytes_accessed=10**6, transcendentals=0),
        name="filters",
    )(filter_first, filter_second)
    lines = (tile_rows + 2 * a) * a + (tile_rows + 2 * b) * b
    side = jax.ShapeDtypeStruct((lines, channels), jnp.float32)
    to_low, to_high = pl.pallas_call(
        pack_kernel,
        out_shape=(side, side),
        in_specs=[IN_VMEM] * 4,
        out_specs=(IN_VMEM, IN_VMEM),
        compiler_params=PARAMS,
        name="pack_sides",
    )(field, cotangent, low, high)
    from_low, from_high = neighbours((to_high, to_low), "y")
    grad = jax.ShapeDtypeStruct((9 * channels, channels), jnp.float32)
    delta_rows = tile_rows + 2
    kept, sent, first_delta = pl.pallas_call(
        functools.partial(main_kernel, height, width),
        out_shape=(
            grad,
            grad,
            jax.ShapeDtypeStruct((2 * SLACK + delta_rows * PITCH, channels), jnp.float32),
        ),
        in_specs=[IN_SMEM] + [IN_VMEM] * 8,
        out_specs=(IN_VMEM, IN_VMEM, IN_VMEM),
        scratch_shapes=[
            image(tile_rows + 2 * a),
            image(tile_rows + 2 * b),
            image(tile_rows + 6),
            image(tile_rows + 6),
            image(tile_rows + 4),
            *parts_scratch(tile_rows + 2 * a),
        ],
        compiler_params=PARAMS,
        name="gradients",
    )(place, field, cotangent, low, high, from_low, from_high, forward, backward)
    first_grad, second_grad = total(kept, sent)
    input_grad = pl.pallas_call(
        input_kernel,
        out_shape=jax.ShapeDtypeStruct(field.shape, jnp.float32),
        in_specs=[IN_VMEM] * 2,
        out_specs=IN_VMEM,
        scratch_shapes=parts_scratch(delta_rows),
        compiler_params=PARAMS,
        cost_estimate=pl.CostEstimate(flops=2 * 10**9, bytes_accessed=10**6, transcendentals=0),
        name="input_grad",
    )(first_delta, backward)
    shape = filter_first.shape
    return (input_grad, first_grad.reshape(shape), second_grad.reshape(shape))


def solution(mesh):
    fine = Mesh(mesh.devices.reshape(4, 4, 4, 2, 8), ("x", "zh", "zl", "core", "y"))
    tile = P(ROWS, "y", None)
    return jax.shard_map(
        local, mesh=fine, in_specs=(tile, P(), P(), tile), out_specs=(tile, P(), P()), check_vma=False
    )
```

```python
import functools
import math

import jax
import jax.numpy as jnp
import numpy as np
from jax import lax
from jax.experimental import pallas as pl
from jax.experimental.pallas import tpu as pltpu
from jax.sharding import Mesh, PartitionSpec as P

ROWS = ("x", "zh", "zl", "core")
FIELD_HALO = 4
COT_HALO = 2
PITCH = 48
LEFT = 8
SLACK = 8
VMEM_LIMIT = 24 * 2**20
PARAMS = pltpu.CompilerParams(vmem_limit_bytes=VMEM_LIMIT)
WHOLE = pltpu.CompilerParams(vmem_limit_bytes=58 * 2**20)
IN_VMEM = pl.BlockSpec(memory_space=pltpu.VMEM)
IN_HBM = pl.BlockSpec(memory_space=pltpu.HBM)
IN_SMEM = pl.BlockSpec(memory_space=pltpu.SMEM)


def neighbours(values, axis):
    count = lax.axis_size(axis)
    forward = [(i, i + 1) for i in range(count - 1)]
    backward = [(target, source) for source, target in forward]
    low, high = values
    return lax.ppermute(low, axis, forward), lax.ppermute(high, axis, backward)


def together(pairs, sems):
    copies = [
        pltpu.make_async_copy(source, target, sems.at[i]) for i, (source, target) in enumerate(pairs)
    ]
    for copy in copies:
        copy.start()
    return copies


def edges_kernel(field, cot, own_field, own_cot, down, up, sems):
    a, b = FIELD_HALO, COT_HALO
    rows = field.shape[0]
    copies = together(
        (
            (field.at[rows - a : rows], down.at[0:a]),
            (cot.at[rows - b : rows], down.at[a : a + b]),
            (field.at[0:a], up.at[0:a]),
            (cot.at[0:b], up.at[a : a + b]),
            (field, own_field),
            (cot, own_cot),
        ),
        sems,
    )
    for copy in copies:
        copy.wait()


def results_kernel(place, mine, theirs, first, second, sems):
    parts = 3
    size = mine.shape[0] // parts

    def put(first_source, second_source):
        pairs = []
        for part in range(parts):
            span = slice(part * size, part * size + size)
            pairs.append((first_source.at[span], first.at[span]))
            pairs.append((second_source.at[span], second.at[span]))
        for copy in together(pairs, sems):
            copy.wait()

    @pl.when(place[2] == 0)
    def _():
        put(theirs, mine)

    @pl.when(place[2] != 0)
    def _():
        put(mine, theirs)


def image(rows, dtype=jnp.float32):
    return pltpu.VMEM((2 * SLACK + rows * PITCH, 128), dtype)


def spot(row, col):
    return SLACK + row * PITCH + col


def pack_kernel(field, cot, low, high, to_low, to_high):
    a, b = FIELD_HALO, COT_HALO
    tile_rows, tile_cols, _ = field.shape
    for out, col_a, col_b in ((to_low, 0, 0), (to_high, tile_cols - a, tile_cols - b)):
        at = 0
        for part, rows, col, count in (
            (low, range(a), col_a, a),
            (field, range(tile_rows), col_a, a),
            (high, range(a), col_a, a),
            (low, range(a, a + b), col_b, b),
            (cot, range(tile_rows), col_b, b),
            (high, range(a, a + b), col_b, b),
        ):
            for row in rows:
                out[at : at + count, :] = part[row, col : col + count, :]
                at += count


def split(values):
    high = values.astype(jnp.bfloat16)
    low = (values - high.astype(jnp.float32)).astype(jnp.bfloat16)
    return high, low


def filters_kernel(filter_first, filter_second, forward, back, held, sems):
    sources = (filter_first, filter_second)
    copies = together(
        [(source.at[a], held.at[layer, a]) for layer, source in enumerate(sources) for a in range(3)],
        sems,
    )
    for layer in range(2):
        source = held.at[layer]
        for a in range(3):
            copies[3 * layer + a].wait()
        for a in range(3):
            taps = source[a].reshape(-1, source.shape[3])
            forward[layer, a] = jnp.concatenate(split(taps), axis=1)
            taps = jnp.concatenate([source[2 - a, 2 - b] for b in range(3)], axis=1)
            back[layer, a] = jnp.concatenate(split(taps), axis=0)


def convolve(source, rows, flip, both, high, low):
    taken = (rows + 2) * PITCH
    made = rows * PITCH
    shifts = [source[SLACK - 1 + b : SLACK - 1 + b + taken, :] for b in range(3)]
    for b in range(3):
        part_high, part_low = split(shifts[b])
        high[0:taken, 128 * b : 128 * b + 128] = part_high
        low[0:taken, 128 * b : 128 * b + 128] = part_low
    dims = (((1,), (1 if flip else 0,)), ((), ()))
    wide = None
    thin = None
    for a in range(3):
        start = a * PITCH
        p = lax.dot_general(
            high[start : start + made, :], both[a], dims, preferred_element_type=jnp.float32
        )
        q = lax.dot_general(
            low[start : start + made, :],
            both[a, :128] if flip else both[a, :, :128],
            dims,
            preferred_element_type=jnp.float32,
        )
        wide = p if wide is None else wide + p
        thin = q if thin is None else thin + q
    return wide[:, :128] + wide[:, 128:] + thin


def filter_product(values, value_row, deltas, delta_row, tile_rows, tile_cols, factor):
    rows = tile_rows + 2
    windows = []
    for b in range(3):
        col = LEFT - 1 + b
        windows.append(
            jnp.concatenate(
                [
                    values[spot(value_row + r, col) : spot(value_row + r, col) + tile_cols, :]
                    for r in range(rows)
                ],
                axis=0,
            )
        )
    high, low = split(jnp.concatenate(windows, axis=1))
    delta = jnp.concatenate(
        [
            deltas[spot(delta_row + r, LEFT) : spot(delta_row + r, LEFT) + tile_cols, :]
            for r in range(tile_rows)
        ],
        axis=0,
    )
    delta_high, delta_low = split((delta * factor).T)
    pixels = tile_rows * tile_cols
    outs = []
    for a in range(3):
        start = a * tile_cols
        window = high[start : start + pixels]
        out = jnp.dot(delta_high, window, preferred_element_type=jnp.float32)
        out += jnp.dot(
            delta_high, low[start : start + pixels], preferred_element_type=jnp.float32
        )
        out += jnp.dot(delta_low, window, preferred_element_type=jnp.float32)
        outs.append(out.T)
    return jnp.concatenate(outs, axis=0)


def inside(place, rows, margin, tile_rows, tile_cols, height, width):
    shape = (rows, PITCH, 128)
    row = lax.broadcasted_iota(jnp.int32, shape, 0) + (place[0] * tile_rows - margin)
    col = lax.broadcasted_iota(jnp.int32, shape, 1) + (place[1] * tile_cols - LEFT)
    keep = (row >= 0) & (row < height) & (col >= 0) & (col < width)
    return jnp.where(keep, 1.0, 0.0).reshape(rows * PITCH, 128) > 0.5


def main_kernel(
    height, width, place, field, cot, low, high, from_low, from_high, forward, backward,
    kept, sent, first_delta_out,
    field_image, cot_image, hidden_image, slope_image, delta_image,
    part_high, part_low,
):
    a, b = FIELD_HALO, COT_HALO
    tile_rows, tile_cols, _ = field.shape
    for target, own, halo, base, offset in (
        (field_image, field, a, 0, 0),
        (cot_image, cot, b, a, (tile_rows + 2 * a) * a),
    ):
        for row in range(tile_rows + 2 * halo):
            if row < halo:
                line = low[base + row]
            elif row < halo + tile_rows:
                line = own[row - halo]
            else:
                line = high[base + row - halo - tile_rows]
            target[spot(row, LEFT) : spot(row, LEFT) + tile_cols, :] = line
            left = spot(row, LEFT - halo)
            target[left : left + halo, :] = from_low[offset + row * halo : offset + row * halo + halo, :]
            right = spot(row, LEFT + tile_cols)
            target[right : right + halo, :] = from_high[
                offset + row * halo : offset + row * halo + halo, :
            ]
    grid = (tile_rows, tile_cols, height, width)
    factor = 1.0 / math.sqrt(height * width)
    core = place[2]

    rows = tile_rows + 6
    pre = convolve(field_image, rows, False, forward.at[0], part_high, part_low)
    sigmoid = jax.nn.sigmoid(pre)
    slope_image[SLACK : SLACK + rows * PITCH, :] = sigmoid * (1.0 + pre * (1.0 - sigmoid))
    hidden_image[SLACK : SLACK + rows * PITCH, :] = jnp.where(
        inside(place, rows, 3, *grid), pre * sigmoid, 0.0
    )

    rows = tile_rows + 4
    pre = convolve(hidden_image, rows, False, forward.at[1], part_high, part_low)
    sigmoid = jax.nn.sigmoid(pre)
    delta_image[SLACK : SLACK + rows * PITCH, :] = cot_image[SLACK : SLACK + rows * PITCH, :] * (
        sigmoid * (1.0 + pre * (1.0 - sigmoid))
    )
    grad = filter_product(hidden_image, 2, delta_image, 2, tile_rows, tile_cols, factor)

    @pl.when(core == 0)
    def _():
        kept[...] = grad

    @pl.when(core != 0)
    def _():
        sent[...] = grad

    rows = tile_rows + 2
    back = convolve(delta_image, rows, True, backward.at[1], part_high, part_low)
    start = spot(2, 0)
    first_delta_out[SLACK : SLACK + rows * PITCH, :] = jnp.where(
        inside(place, rows, 1, *grid), back * slope_image[start : start + rows * PITCH, :], 0.0
    )
    grad = filter_product(field_image, 3, first_delta_out, 1, tile_rows, tile_cols, factor)

    @pl.when(core == 0)
    def _():
        sent[...] = grad

    @pl.when(core != 0)
    def _():
        kept[...] = grad


def input_kernel(first_delta, backward, input_grad, part_high, part_low):
    tile_rows, tile_cols, _ = input_grad.shape
    out = convolve(first_delta, tile_rows, True, backward.at[0], part_high, part_low)
    for row in range(tile_rows):
        start = row * PITCH + LEFT
        input_grad[row] = out[start : start + tile_cols]


def parts_scratch(rows):
    return [pltpu.VMEM((rows * PITCH, 384), jnp.bfloat16)] * 2


ALL = ("x", "zh", "zl", "core", "y")


def groups(kinds):
    sizes = [lax.axis_size(axis) for axis in ALL[:4]] + [lax.axis_size("y") // 2, 2]
    names = ["x", "zh", "zl", "core", "yh", "yl"]
    ids = np.arange(math.prod(sizes)).reshape(sizes)
    found = []
    for core, inner in enumerate(kinds):
        outer = [name for name in names if name not in inner]
        order = [names.index(name) for name in outer + list(inner)]
        moved = np.take(ids, [core], axis=3).transpose(order)
        found.append(moved.reshape(-1, math.prod(sizes[names.index(name)] for name in inner)))
    return np.concatenate(found).tolist()


def exchange(parts, kinds):
    return lax.all_to_all(parts, ALL, 0, 0, axis_index_groups=groups(kinds))


def to_all(values, kinds):
    count = len(groups(kinds)[0])
    return exchange(jnp.broadcast_to(values[None], (count,) + values.shape), kinds)


def total(mine, theirs):
    other = [(0, 1), (1, 0)]
    plane = (("x", "yh", "yl"), ("x", "zl", "yl"))
    with jax.named_scope("cores"):
        mine = mine + lax.ppermute(theirs, "core", other)
    channels = mine.shape[-1]
    with jax.named_scope("plane_scatter"):
        n = len(groups(plane)[0])
        mine = exchange(mine.reshape(n, -1, channels), plane).sum(0)
    with jax.named_scope("rest_total"):
        mine = to_all(mine, (("zl",), ("yh",))).sum(0)
        mine = to_all(mine, (("zh",), ("zh",))).sum(0)
    with jax.named_scope("plane_gather"):
        mine = to_all(mine, plane).reshape(-1, channels)
    with jax.named_scope("cores_back"):
        theirs = lax.ppermute(mine, "core", other)
    return mine, theirs


def local(field, filter_first, filter_second, cotangent):
    tile_rows, tile_cols, channels = field.shape
    a, b = FIELD_HALO, COT_HALO
    height = tile_rows * lax.axis_size(ROWS)
    width = tile_cols * lax.axis_size("y")
    place = jnp.stack([lax.axis_index(ROWS), lax.axis_index("y"), lax.axis_index("core")])
    place = place.astype(jnp.int32)
    edge = jax.ShapeDtypeStruct((a + b, tile_cols, channels), jnp.float32)
    tile = jax.ShapeDtypeStruct(field.shape, jnp.float32)
    field, cotangent, down, up = pl.pallas_call(
        edges_kernel,
        out_shape=(tile, tile, edge, edge),
        in_specs=[IN_HBM] * 2,
        out_specs=(IN_VMEM,) * 4,
        scratch_shapes=[pltpu.SemaphoreType.DMA((6,))],
        compiler_params=WHOLE,
        name="edges",
    )(field, cotangent)
    low, high = neighbours((down, up), ROWS)
    forward, backward = pl.pallas_call(
        filters_kernel,
        out_shape=(
            jax.ShapeDtypeStruct((2, 3, 3 * channels, 2 * channels), jnp.bfloat16),
            jax.ShapeDtypeStruct((2, 3, 2 * channels, 3 * channels), jnp.bfloat16),
        ),
        in_specs=[IN_HBM] * 2,
        out_specs=(IN_VMEM, IN_VMEM),
        scratch_shapes=[
            pltpu.VMEM((2,) + filter_first.shape, jnp.float32),
            pltpu.SemaphoreType.DMA((6,)),
        ],
        compiler_params=WHOLE,
        cost_estimate=pl.CostEstimate(flops=2 * 10**9, bytes_accessed=10**6, transcendentals=0),
        name="filters",
    )(filter_first, filter_second)
    lines = (tile_rows + 2 * a) * a + (tile_rows + 2 * b) * b
    side = jax.ShapeDtypeStruct((lines, channels), jnp.float32)
    to_low, to_high = pl.pallas_call(
        pack_kernel,
        out_shape=(side, side),
        in_specs=[IN_VMEM] * 4,
        out_specs=(IN_VMEM, IN_VMEM),
        compiler_params=PARAMS,
        name="pack_sides",
    )(field, cotangent, low, high)
    from_low, from_high = neighbours((to_high, to_low), "y")
    grad = jax.ShapeDtypeStruct((9 * channels, channels), jnp.float32)
    delta_rows = tile_rows + 2
    kept, sent, first_delta = pl.pallas_call(
        functools.partial(main_kernel, height, width),
        out_shape=(
            grad,
            grad,
            jax.ShapeDtypeStruct((2 * SLACK + delta_rows * PITCH, channels), jnp.float32),
        ),
        in_specs=[IN_SMEM] + [IN_VMEM] * 8,
        out_specs=(IN_VMEM, IN_VMEM, IN_VMEM),
        scratch_shapes=[
            image(tile_rows + 2 * a),
            image(tile_rows + 2 * b),
            image(tile_rows + 6),
            image(tile_rows + 6),
            image(tile_rows + 4),
            *parts_scratch(tile_rows + 2 * a),
        ],
        compiler_params=PARAMS,
        name="gradients",
    )(place, field, cotangent, low, high, from_low, from_high, forward, backward)
    mine, theirs = total(kept, sent)
    input_grad = pl.pallas_call(
        input_kernel,
        out_shape=jax.ShapeDtypeStruct(field.shape, jnp.float32),
        in_specs=[IN_VMEM] * 2,
        out_specs=IN_VMEM,
        scratch_shapes=parts_scratch(delta_rows),
        compiler_params=PARAMS,
        cost_estimate=pl.CostEstimate(flops=2 * 10**9, bytes_accessed=10**6, transcendentals=0),
        name="input_grad",
    )(first_delta, backward)
    first_grad, second_grad = pl.pallas_call(
        results_kernel,
        out_shape=(grad, grad),
        in_specs=[IN_SMEM, IN_VMEM, IN_VMEM],
        out_specs=(IN_HBM, IN_HBM),
        scratch_shapes=[pltpu.SemaphoreType.DMA((6,))],
        compiler_params=PARAMS,
        name="results",
    )(place, mine, theirs)
    shape = filter_first.shape
    return (input_grad, first_grad.reshape(shape), second_grad.reshape(shape))


def solution(mesh):
    fine = Mesh(mesh.devices.reshape(4, 4, 4, 2, 8), ("x", "zh", "zl", "core", "y"))
    tile = P(ROWS, "y", None)
    return jax.shard_map(
        local, mesh=fine, in_specs=(tile, P(), P(), tile), out_specs=(tile, P(), P()), check_vma=False
    )
```

```python
import functools
import math

import jax
import jax.numpy as jnp
import numpy as np
from jax import lax
from jax.experimental import pallas as pl
from jax.experimental.pallas import tpu as pltpu
from jax.sharding import Mesh, PartitionSpec as P

ROWS = ("x", "zh", "zl", "core")
FIELD_HALO = 4
COT_HALO = 2
PITCH = 48
LEFT = 8
SLACK = 8
VMEM_LIMIT = 24 * 2**20
PARAMS = pltpu.CompilerParams(vmem_limit_bytes=VMEM_LIMIT)
IN_VMEM = pl.BlockSpec(memory_space=pltpu.VMEM)
IN_SMEM = pl.BlockSpec(memory_space=pltpu.SMEM)


def neighbours(values, axis):
    count = lax.axis_size(axis)
    forward = [(i, i + 1) for i in range(count - 1)]
    backward = [(target, source) for source, target in forward]
    low, high = values
    return lax.ppermute(low, axis, forward), lax.ppermute(high, axis, backward)


def image(rows, dtype=jnp.float32):
    return pltpu.VMEM((2 * SLACK + rows * PITCH, 128), dtype)


def spot(row, col):
    return SLACK + row * PITCH + col


def pack_kernel(field, cot, low, high, to_low, to_high):
    a, b = FIELD_HALO, COT_HALO
    tile_rows, tile_cols, _ = field.shape
    for out, col_a, col_b in ((to_low, 0, 0), (to_high, tile_cols - a, tile_cols - b)):
        at = 0
        for part, rows, col, count in (
            (low, range(a), col_a, a),
            (field, range(tile_rows), col_a, a),
            (high, range(a), col_a, a),
            (low, range(a, a + b), col_b, b),
            (cot, range(tile_rows), col_b, b),
            (high, range(a, a + b), col_b, b),
        ):
            for row in rows:
                out[at : at + count, :] = part[row, col : col + count, :]
                at += count


def split(values):
    high = values.astype(jnp.bfloat16)
    low = (values - high.astype(jnp.float32)).astype(jnp.bfloat16)
    return high, low


def filters_kernel(filter_first, filter_second, forward, back):
    for layer, source in enumerate((filter_first, filter_second)):
        for a in range(3):
            taps = source[a].reshape(-1, source.shape[3])
            forward[layer, a] = jnp.concatenate(split(taps), axis=1)
            taps = jnp.concatenate([source[2 - a, 2 - b] for b in range(3)], axis=1)
            back[layer, a] = jnp.concatenate(split(taps), axis=0)


def convolve(source, rows, flip, both, high, low):
    taken = (rows + 2) * PITCH
    made = rows * PITCH
    shifts = [source[SLACK - 1 + b : SLACK - 1 + b + taken, :] for b in range(3)]
    for b in range(3):
        part_high, part_low = split(shifts[b])
        high[0:taken, 128 * b : 128 * b + 128] = part_high
        low[0:taken, 128 * b : 128 * b + 128] = part_low
    dims = (((1,), (1 if flip else 0,)), ((), ()))
    wide = None
    thin = None
    for a in range(3):
        start = a * PITCH
        p = lax.dot_general(
            high[start : start + made, :], both[a], dims, preferred_element_type=jnp.float32
        )
        q = lax.dot_general(
            low[start : start + made, :],
            both[a, :128] if flip else both[a, :, :128],
            dims,
            preferred_element_type=jnp.float32,
        )
        wide = p if wide is None else wide + p
        thin = q if thin is None else thin + q
    return wide[:, :128] + wide[:, 128:] + thin


def filter_product(values, value_row, deltas, delta_row, tile_rows, tile_cols, factor):
    rows = tile_rows + 2
    windows = []
    for b in range(3):
        col = LEFT - 1 + b
        windows.append(
            jnp.concatenate(
                [
                    values[spot(value_row + r, col) : spot(value_row + r, col) + tile_cols, :]
                    for r in range(rows)
                ],
                axis=0,
            )
        )
    high, low = split(jnp.concatenate(windows, axis=1))
    delta = jnp.concatenate(
        [
            deltas[spot(delta_row + r, LEFT) : spot(delta_row + r, LEFT) + tile_cols, :]
            for r in range(tile_rows)
        ],
        axis=0,
    )
    delta_high, delta_low = split((delta * factor).T)
    pixels = tile_rows * tile_cols
    outs = []
    for a in range(3):
        start = a * tile_cols
        window = high[start : start + pixels]
        out = jnp.dot(delta_high, window, preferred_element_type=jnp.float32)
        out += jnp.dot(
            delta_high, low[start : start + pixels], preferred_element_type=jnp.float32
        )
        out += jnp.dot(delta_low, window, preferred_element_type=jnp.float32)
        outs.append(out.T)
    return jnp.concatenate(outs, axis=0)


def inside(place, rows, margin, tile_rows, tile_cols, height, width):
    shape = (rows, PITCH, 128)
    row = lax.broadcasted_iota(jnp.int32, shape, 0) + (place[0] * tile_rows - margin)
    col = lax.broadcasted_iota(jnp.int32, shape, 1) + (place[1] * tile_cols - LEFT)
    keep = (row >= 0) & (row < height) & (col >= 0) & (col < width)
    return jnp.where(keep, 1.0, 0.0).reshape(rows * PITCH, 128) > 0.5


def main_kernel(
    height, width, place, field, cot, low, high, from_low, from_high, forward, backward,
    kept, sent, first_delta_out,
    field_image, cot_image, hidden_image, slope_image, delta_image,
    part_high, part_low,
):
    a, b = FIELD_HALO, COT_HALO
    tile_rows, tile_cols, _ = field.shape
    for target, own, halo, base, offset in (
        (field_image, field, a, 0, 0),
        (cot_image, cot, b, a, (tile_rows + 2 * a) * a),
    ):
        for row in range(tile_rows + 2 * halo):
            if row < halo:
                line = low[base + row]
            elif row < halo + tile_rows:
                line = own[row - halo]
            else:
                line = high[base + row - halo - tile_rows]
            target[spot(row, LEFT) : spot(row, LEFT) + tile_cols, :] = line
            left = spot(row, LEFT - halo)
            target[left : left + halo, :] = from_low[offset + row * halo : offset + row * halo + halo, :]
            right = spot(row, LEFT + tile_cols)
            target[right : right + halo, :] = from_high[
                offset + row * halo : offset + row * halo + halo, :
            ]
    grid = (tile_rows, tile_cols, height, width)
    factor = 1.0 / math.sqrt(height * width)
    core = place[2]

    rows = tile_rows + 6
    pre = convolve(field_image, rows, False, forward.at[0], part_high, part_low)
    sigmoid = jax.nn.sigmoid(pre)
    slope_image[SLACK : SLACK + rows * PITCH, :] = sigmoid * (1.0 + pre * (1.0 - sigmoid))
    hidden_image[SLACK : SLACK + rows * PITCH, :] = jnp.where(
        inside(place, rows, 3, *grid), pre * sigmoid, 0.0
    )

    rows = tile_rows + 4
    pre = convolve(hidden_image, rows, False, forward.at[1], part_high, part_low)
    sigmoid = jax.nn.sigmoid(pre)
    delta_image[SLACK : SLACK + rows * PITCH, :] = cot_image[SLACK : SLACK + rows * PITCH, :] * (
        sigmoid * (1.0 + pre * (1.0 - sigmoid))
    )
    grad = filter_product(hidden_image, 2, delta_image, 2, tile_rows, tile_cols, factor)

    @pl.when(core == 0)
    def _():
        kept[...] = grad

    @pl.when(core != 0)
    def _():
        sent[...] = grad

    rows = tile_rows + 2
    back = convolve(delta_image, rows, True, backward.at[1], part_high, part_low)
    start = spot(2, 0)
    first_delta_out[SLACK : SLACK + rows * PITCH, :] = jnp.where(
        inside(place, rows, 1, *grid), back * slope_image[start : start + rows * PITCH, :], 0.0
    )
    grad = filter_product(field_image, 3, first_delta_out, 1, tile_rows, tile_cols, factor)

    @pl.when(core == 0)
    def _():
        sent[...] = grad

    @pl.when(core != 0)
    def _():
        kept[...] = grad


def input_kernel(first_delta, backward, input_grad, part_high, part_low):
    tile_rows, tile_cols, _ = input_grad.shape
    out = convolve(first_delta, tile_rows, True, backward.at[0], part_high, part_low)
    for row in range(tile_rows):
        start = row * PITCH + LEFT
        input_grad[row] = out[start : start + tile_cols]


def parts_scratch(rows):
    return [pltpu.VMEM((rows * PITCH, 384), jnp.bfloat16)] * 2


ALL = ("x", "zh", "zl", "core", "y")


def groups(kinds):
    sizes = [lax.axis_size(axis) for axis in ALL[:4]] + [lax.axis_size("y") // 2, 2]
    names = ["x", "zh", "zl", "core", "yh", "yl"]
    ids = np.arange(math.prod(sizes)).reshape(sizes)
    found = []
    for core, inner in enumerate(kinds):
        outer = [name for name in names if name not in inner]
        order = [names.index(name) for name in outer + list(inner)]
        moved = np.take(ids, [core], axis=3).transpose(order)
        found.append(moved.reshape(-1, math.prod(sizes[names.index(name)] for name in inner)))
    return np.concatenate(found).tolist()


def exchange(parts, kinds):
    return lax.all_to_all(parts, ALL, 0, 0, axis_index_groups=groups(kinds))


def to_all(values, kinds):
    count = len(groups(kinds)[0])
    return exchange(jnp.broadcast_to(values[None], (count,) + values.shape), kinds)


def total(mine, theirs):
    other = [(0, 1), (1, 0)]
    plane = (("x", "yh", "yl"), ("x", "zl", "yl"))
    with jax.named_scope("cores"):
        mine = mine + lax.ppermute(theirs, "core", other)
    channels = mine.shape[-1]
    with jax.named_scope("plane_scatter"):
        n = len(groups(plane)[0])
        mine = exchange(mine.reshape(n, -1, channels), plane).sum(0)
    with jax.named_scope("rest_total"):
        mine = to_all(mine, (("zl",), ("yh",))).sum(0)
        mine = to_all(mine, (("zh",), ("zh",))).sum(0)
    with jax.named_scope("plane_gather"):
        mine = to_all(mine, plane).reshape(-1, channels)
    with jax.named_scope("cores_back"):
        theirs = lax.ppermute(mine, "core", other)
    return mine, theirs


def local(field, filter_first, filter_second, cotangent):
    tile_rows, tile_cols, channels = field.shape
    a, b = FIELD_HALO, COT_HALO
    height = tile_rows * lax.axis_size(ROWS)
    width = tile_cols * lax.axis_size("y")
    place = jnp.stack([lax.axis_index(ROWS), lax.axis_index("y"), lax.axis_index("core")])
    place = place.astype(jnp.int32)
    low, high = neighbours(
        (
            jnp.concatenate([field[-a:], cotangent[-b:]], axis=0),
            jnp.concatenate([field[:a], cotangent[:b]], axis=0),
        ),
        ROWS,
    )
    forward, backward = pl.pallas_call(
        filters_kernel,
        out_shape=(
            jax.ShapeDtypeStruct((2, 3, 3 * channels, 2 * channels), jnp.bfloat16),
            jax.ShapeDtypeStruct((2, 3, 2 * channels, 3 * channels), jnp.bfloat16),
        ),
        in_specs=[IN_VMEM] * 2,
        out_specs=(IN_VMEM, IN_VMEM),
        compiler_params=PARAMS,
        cost_estimate=pl.CostEstimate(flops=2 * 10**9, bytes_accessed=10**6, transcendentals=0),
        name="filters",
    )(filter_first, filter_second)
    lines = (tile_rows + 2 * a) * a + (tile_rows + 2 * b) * b
    side = jax.ShapeDtypeStruct((lines, channels), jnp.float32)
    to_low, to_high = pl.pallas_call(
        pack_kernel,
        out_shape=(side, side),
        in_specs=[IN_VMEM] * 4,
        out_specs=(IN_VMEM, IN_VMEM),
        compiler_params=PARAMS,
        name="pack_sides",
    )(field, cotangent, low, high)
    from_low, from_high = neighbours((to_high, to_low), "y")
    grad = jax.ShapeDtypeStruct((9 * channels, channels), jnp.float32)
    delta_rows = tile_rows + 2
    kept, sent, first_delta = pl.pallas_call(
        functools.partial(main_kernel, height, width),
        out_shape=(
            grad,
            grad,
            jax.ShapeDtypeStruct((2 * SLACK + delta_rows * PITCH, channels), jnp.float32),
        ),
        in_specs=[IN_SMEM] + [IN_VMEM] * 8,
        out_specs=(IN_VMEM, IN_VMEM, IN_VMEM),
        scratch_shapes=[
            image(tile_rows + 2 * a),
            image(tile_rows + 2 * b),
            image(tile_rows + 6),
            image(tile_rows + 6),
            image(tile_rows + 4),
            *parts_scratch(tile_rows + 2 * a),
        ],
        compiler_params=PARAMS,
        name="gradients",
    )(place, field, cotangent, low, high, from_low, from_high, forward, backward)
    mine, theirs = total(kept, sent)
    holds_second = place[2] == 0
    first_grad = jnp.where(holds_second, theirs, mine)
    second_grad = jnp.where(holds_second, mine, theirs)
    input_grad = pl.pallas_call(
        input_kernel,
        out_shape=jax.ShapeDtypeStruct(field.shape, jnp.float32),
        in_specs=[IN_VMEM] * 2,
        out_specs=IN_VMEM,
        scratch_shapes=parts_scratch(delta_rows),
        compiler_params=PARAMS,
        cost_estimate=pl.CostEstimate(flops=2 * 10**9, bytes_accessed=10**6, transcendentals=0),
        name="input_grad",
    )(first_delta, backward)
    shape = filter_first.shape
    return (input_grad, first_grad.reshape(shape), second_grad.reshape(shape))


def solution(mesh):
    fine = Mesh(mesh.devices.reshape(4, 4, 4, 2, 8), ("x", "zh", "zl", "core", "y"))
    tile = P(ROWS, "y", None)
    return jax.shard_map(
        local, mesh=fine, in_specs=(tile, P(), P(), tile), out_specs=(tile, P(), P()), check_vma=False
    )
```
